32 devices in a mesh: grp: 2 (over y), field: 4 (over z), pair: 4 (over x, core).
Axes of the slice: x: 2, y: 2, z: 4, core: 2. Of those that a mesh axis runs over, the one named last changes fastest.
Arguments:
- cholesky_tensor: float32 [1536, 9216], P(('grp', 'field'), 'pair'), parts along dimension 0, may hold values from -0.0625 to 0.0625
- green_function: float32 [2, 8192, 9216], P(None, ('grp', 'field'), 'pair'), parts along dimension 1, may hold values from -6 to 6
- mean_field: float32 [2, 1536], P(None, 'grp'), parts along dimension 1, may hold values from -6 to 6
- field_noise: float32 [8192, 768], P(('grp', 'field')), parts along dimension 0, may hold values from -6 to 6
Outputs:
- capped_bias: float32 [2, 8192, 768], P(None, ('grp', 'field', 'pair')), parts along dimension 1
- one_body: float32 [8192, 2, 9216], P(('grp', 'field'), None, 'pair'), parts along dimension 0
The draws below stay inside these ranges and needn't reach their ends.
There are 2 independent parts, one for each index of `grp`. The reference program is written for one: setup_inputs(seed, part) draws one part's arguments, and reference() takes and returns one part's arrays. A program takes and returns all parts, laid end to end along the dimension named above; each array names one. Nothing has to cross between parts.
All inputs are finite; a program needn't handle non-finite values.
Results may differ from the reference program's by a relative error of at most 0.000059.
Values sent between devices are 32-bit elements; how exact they have to be, the bound alone decides.
No kernel may reach another device: no remote copies, remote signals or barrier semaphores. Data moves between devices by JAX's collectives and lax.ppermute only.
A program may use at most 128 MiB of HBM per device.

```python
import math
import jax
import jax.numpy as jnp
from jax import lax

NF = 768
NP = 9216
WALK = 4096


def steps_of(own_key, extent, cuts, least, largest):
    loudness, own = 1.0, jax.random.fold_in(own_key, 6)
    for dim, blocks in cuts:
        draws = jnp.exp(jax.random.uniform(jax.random.fold_in(own, dim), (blocks,), jnp.float32, least / len(cuts), largest / len(cuts)))
        loudness = loudness * jnp.repeat(draws, extent[dim] // blocks).reshape([-1 if axis == dim else 1 for axis in range(len(extent))])
    return loudness


def noise(own_key, dims, deviation, bound, shards=(), kind=jnp.bfloat16):
    factor_of = steps_of(own_key, dims, shards, -0.22, 0.18) if shards else 1.0
    drawn = jax.random.normal(own_key, dims, jnp.float32) * deviation * factor_of
    return jnp.minimum(jnp.maximum(drawn, -bound), bound).astype(kind)


def setup_inputs(seed: int = 0, part: int = 0) -> dict:
    keys = jax.random.split(jax.random.key(seed), 5)
    own_keys = jax.random.split(jax.random.fold_in(keys[4], part), 5)
    cholesky_tensor = noise(own_keys[0], (NF, NP), NP ** -0.5, 0.0625, ((0, 4), (1, 4)), jnp.float32)
    green_function = noise(own_keys[1], (2, WALK, NP), 1.0, 6.0, ((1, 4), (2, 4)), jnp.float32)
    mean_field = noise(own_keys[2], (2, NF), 1.0, 6.0, (), jnp.float32)
    field_noise = noise(own_keys[3], (WALK, NF), 1.0, 6.0, ((0, 4),), jnp.float32)
    return {"cholesky_tensor": cholesky_tensor, "green_function": green_function, "mean_field": mean_field, "field_noise": field_noise}


def reference(cholesky_tensor, green_function, mean_field, field_noise):
    bias = jnp.einsum('cwp,fp->cwf', green_function, cholesky_tensor, precision=lax.Precision.HIGHEST)
    shifted = bias - mean_field[:, None, :]
    capped = 2.0 * jnp.tanh(shifted / 2.0)
    fields = jnp.stack([field_noise - capped[0], -capped[1]], axis=1)
    operator_scale = math.sqrt(NP / NF)
    one_body = operator_scale * jnp.einsum('wcf,fp->wcp', fields, cholesky_tensor, precision=lax.Precision.HIGHEST)
    return (capped, one_body)
```

```python
import functools
import math

import jax
import jax.numpy as jnp
from jax import lax
from jax.experimental import pallas as pl
from jax.experimental.pallas import tpu as pltpu
from jax.sharding import PartitionSpec as P

CORES = 2
KERNEL_VMEM = 24 * 1024 * 1024
ROWS_DOT = (((1,), (1,)), ((), ()))
DOT = (((1,), (0,)), ((), ()))
WHOLE = pl.BlockSpec(memory_space=pltpu.VMEM)


def split(x):
    high = x.astype(jnp.bfloat16)
    return high, (x - high.astype(jnp.float32)).astype(jnp.bfloat16)


def params():
    return pltpu.CompilerParams(vmem_limit_bytes=KERNEL_VMEM)


def stacked(parts):
    return parts[0] if len(parts) == 1 else jnp.concatenate(parts, 0)


def split_green_kernel(green_ref, high_ref, low_ref):
    at = (pl.program_id(0), pl.program_id(1), pl.program_id(2))
    high_ref[at], low_ref[at] = split(green_ref[0, 0, 0])


def split_green(green):
    channels, across, cores, rows, pairs = green.shape
    return pl.pallas_call(
        split_green_kernel,
        out_shape=[pltpu.VMEM(green.shape, jnp.bfloat16)] * 2,
        grid=(channels, across, cores),
        in_specs=[pl.BlockSpec((1, 1, 1, rows, pairs), lambda c, x, h: (c, x, h, 0, 0))],
        out_specs=[WHOLE, WHOLE],
        compiler_params=params(),
        cost_estimate=pl.CostEstimate(flops=3 * green.size, bytes_accessed=4 * green.size, transcendentals=0),
        name="split_green",
    )(green)


def bias_kernel(n, half_ref, high_ref, low_ref, *refs):
    parts, out_ref, chol = refs[:n], refs[n], refs[n + 1]
    fields = chol.shape[0] // 2
    chol[:fields], chol[fields:] = split(stacked([part[...] for part in parts]))
    channels, across = high_ref.shape[:2]
    half = half_ref[0]
    for c in range(channels):
        for x in range(across):
            both = lax.dot_general(chol[...], high_ref[c, x, half], ROWS_DOT, preferred_element_type=jnp.float32)
            cross = lax.dot_general(chol[:fields], low_ref[c, x, half], ROWS_DOT, preferred_element_type=jnp.float32)
            out_ref[c, x] = both[:fields] + (both[fields:] + cross)


def bias_of(high, low, parts, half):
    channels, across, _, rows, pairs = high.shape
    fields = sum(part.shape[0] for part in parts)
    return pl.pallas_call(
        functools.partial(bias_kernel, len(parts)),
        out_shape=jax.ShapeDtypeStruct((channels, across, fields, rows), jnp.float32),
        in_specs=[pl.BlockSpec(memory_space=pltpu.SMEM)] + [WHOLE] * (2 + len(parts)),
        out_specs=WHOLE,
        scratch_shapes=[pltpu.VMEM((2 * fields, pairs), jnp.bfloat16)],
        compiler_params=params(),
        cost_estimate=pl.CostEstimate(
            flops=6 * channels * across * rows * pairs * fields, bytes_accessed=4 * fields * pairs, transcendentals=0
        ),
        name="bias",
    )(half, high, low, *parts)


def stack_chol(out, parts):
    high, low = split(stacked([part[...] for part in parts]))
    depth = high.shape[0]
    out[:depth] = high
    out[depth : 2 * depth] = high
    out[2 * depth :] = low


def stack_fields(capped, noise):
    first = stacked(noise) - stacked([c[0] for c in capped])
    second = -stacked([c[1] for c in capped])
    high, low = split(jnp.concatenate([first, second], 1))
    return jnp.concatenate([high, low, high], 0).T


def noise_specs(unit, lanes, at):
    def spec(step, shard):
        return pl.BlockSpec((1, 1, shard, lanes), lambda x, b, s: (s[1 + step], *at(x, b, s)))

    return [spec(step, shard) for step, _, _, shard in unit]


def noise_pieces(refs, unit):
    return [ref[0, 0, start : start + rows] for ref, (_, start, rows, _) in zip(refs, unit)]


def accumulate_kernel(n, m, unit, old, s_ref, *refs):
    mine, other, noise, chol = refs[:n], refs[n : 2 * n], refs[2 * n : 2 * n + m], refs[2 * n + m : 2 * n + 2 * m]
    out_ref, stack = refs[-2], refs[-1]
    x, core = pl.program_id(0), pl.program_id(1)

    @pl.when((x == 0) & (core == 0))
    def _():
        stack_chol(stack, chol)

    own = core == s_ref[0]
    capped = [jnp.where(own, a[:, 0], b[:, 0]) for a, b in zip(mine, other)]
    sums = lax.dot_general(
        stack_fields(capped, noise_pieces(noise, unit)), stack[...], DOT, preferred_element_type=jnp.float32
    )
    rows = sums.shape[0] // 2
    for c in range(2):
        term = sums[c * rows : (c + 1) * rows]
        out_ref[c, x, core] = term + refs[-3][c, x, core] if old else term


def accumulate(mine, other, noise, chol, unit, scalars, prior, sizes):
    across, rows, pairs = sizes
    depth = sum(part.shape[0] for part in chol)
    in_specs = [pl.BlockSpec((2, 1, *part.shape[2:]), lambda x, b, s: (0, x, 0, 0)) for part in (*mine, *other)]
    in_specs += noise_specs(unit, rows, lambda x, b, s: (x * CORES + b, 0, 0))
    in_specs += [pl.BlockSpec(part.shape, lambda x, b, s: (0, 0)) for part in chol]
    operands = [scalars, *mine, *other, *([noise] * len(unit)), *chol]
    aliases = {}
    if prior is not None:
        in_specs.append(WHOLE)
        aliases = {len(operands): 0}
        operands.append(prior)
    return pl.pallas_call(
        functools.partial(accumulate_kernel, len(mine), len(unit), unit, prior is not None),
        out_shape=pltpu.VMEM((2, across, CORES, rows, pairs), jnp.float32),
        grid_spec=pltpu.PrefetchScalarGridSpec(
            num_scalar_prefetch=1,
            grid=(across, CORES),
            in_specs=in_specs,
            out_specs=WHOLE,
            scratch_shapes=[pltpu.VMEM((3 * depth, pairs), jnp.bfloat16)],
        ),
        input_output_aliases=aliases,
        compiler_params=params(),
        cost_estimate=pl.CostEstimate(
            flops=12 * across * CORES * rows * pairs * depth, bytes_accessed=4 * depth * pairs, transcendentals=0
        ),
        name="accumulate",
    )(*operands)


def stack_kernel(*refs):
    stack_chol(refs[-1], refs[:-1])


def stack_of(chol):
    depth = sum(part.shape[0] for part in chol)
    return pl.pallas_call(
        stack_kernel,
        out_shape=pltpu.VMEM((3 * depth, chol[0].shape[1]), jnp.bfloat16),
        in_specs=[WHOLE] * len(chol),
        out_specs=WHOLE,
        compiler_params=params(),
        name="stack_cholesky",
    )(*chol)


def finish_kernel(n, m, unit, scale, s_ref, *refs):
    capped, noise = refs[:n], refs[n : n + m]
    stack, prior, out_ref = refs[n + m], refs[n + m + 1], refs[-1]
    x, b = pl.program_id(0), pl.program_id(1)
    sums = lax.dot_general(
        stack_fields([part[:, 0] for part in capped], noise_pieces(noise, unit)),
        stack[...],
        DOT,
        preferred_element_type=jnp.float32,
    )
    rows = sums.shape[0] // 2
    at = pl.ds(pl.multiple_of(b * rows, rows), rows)
    for c in range(2):
        out_ref[0, 0, :, c, :] = scale * (prior[c, x, s_ref[0], at, :] + sums[c * rows : (c + 1) * rows])


def finish(capped, noise, stack, prior, unit, scalars, scale, earlier, block):
    _, across, _, rows, pairs = prior.shape
    blocks = rows // block
    in_specs = [pl.BlockSpec((2, 1, part.shape[2], block), lambda x, b, s: (0, x, 0, b)) for part in capped]
    in_specs += noise_specs(unit, block, lambda x, b, s: (x * CORES + s[0], 0, b))
    in_specs += [WHOLE, WHOLE]
    operands = [scalars, *capped, *([noise] * len(unit)), stack, prior]
    aliases = {}
    if earlier is not None:
        in_specs.append(pl.BlockSpec(memory_space=pl.ANY))
        aliases = {len(operands): 0}
        operands.append(earlier)
    return pl.pallas_call(
        functools.partial(finish_kernel, len(capped), len(unit), unit, scale),
        out_shape=jax.ShapeDtypeStruct((across, CORES, rows, 2, pairs), jnp.float32),
        grid_spec=pltpu.PrefetchScalarGridSpec(
            num_scalar_prefetch=1,
            grid=(across, blocks),
            in_specs=in_specs,
            out_specs=pl.BlockSpec((1, 1, block, 2, pairs), lambda x, b, s: (x, s[0], b, 0, 0)),
        ),
        input_output_aliases=aliases,
        compiler_params=params(),
        cost_estimate=pl.CostEstimate(
            flops=4 * across * rows * pairs * stack.shape[0], bytes_accessed=8 * across * rows * pairs, transcendentals=0
        ),
        name="finish",
    )(*operands)


def per_device(ring_size, pair_size, cholesky_tensor, green_function, mean_field, field_noise):
    shard, pairs = cholesky_tensor.shape
    channels, walkers, _ = green_function.shape
    fields = ring_size * shard
    total_pairs = pair_size * pairs
    across = pair_size // CORES
    rows = walkers // pair_size

    place, member = lax.axis_index("field"), lax.axis_index("pair")
    core, chip = member % CORES, member // CORES
    owners = [(place - step) % ring_size for step in range(ring_size)]
    mine_scalars = jnp.stack([core, *owners]).astype(jnp.int32)
    other_scalars = jnp.stack([1 - core, *owners]).astype(jnp.int32)
    own_half, mate_half = mine_scalars[:1], other_scalars[:1]

    ring = [(i, (i + 1) % ring_size) for i in range(ring_size)]
    mates = [(i, i ^ 1) for i in range(pair_size)]

    cut = 2 * shard // 3
    cuts = [(0, cut), (cut, shard - cut)] if cut % 16 == 0 and (shard - cut) % 16 == 0 else [(0, shard)]
    held = [[lax.slice_in_dim(cholesky_tensor, start, start + n, axis=0) for start, n in cuts]]
    for _ in range(ring_size - 1):
        held.append([lax.ppermute(part, "field", ring) for part in held[-1]])
    held[0] = [cholesky_tensor]
    pieces = {0: [(0, 0, shard, shard)]}
    for step in range(1, ring_size):
        pieces[step] = [(step, start, n, shard) for start, n in cuts]

    together = 1
    while together * shard % 16 or (ring_size > 8 and together * 8 < ring_size):
        together *= 2
    units = []
    for first in range(0, ring_size, together):
        steps = range(first, min(first + together, ring_size))
        unit = [(piece, part) for step in steps for piece, part in zip(pieces[step], held[step])]
        last = first + together >= ring_size
        units += [[one] for one in unit] if last and together == 1 else [unit]
    final = len(cuts) if together == 1 else 1

    green = green_function.reshape(channels, across, CORES, rows, pairs)
    high, low = split_green(green)
    noise = field_noise.reshape(pair_size, rows, ring_size, shard).transpose(2, 0, 3, 1)
    means = mean_field.reshape(channels, ring_size, shard)

    def mean_of(piece):
        step, start, n, _ = piece
        return lax.dynamic_index_in_dim(means, owners[step], 1, keepdims=False)[:, start : start + n]

    def capped_of(unit):
        parts = [part for _, part in unit]
        sent = bias_of(high, low, parts, mate_half)
        arrived = lax.ppermute(sent, "pair", mates)
        sums = bias_of(high, low, parts, own_half) + arrived
        reach = CORES
        while reach < pair_size:
            sums = sums + lax.ppermute(sums, "pair", [(i, i ^ reach) for i in range(pair_size)])
            reach *= 2
        mean = jnp.concatenate([mean_of(piece) for piece, _ in unit], 1)[:, None, :, None]
        mine = 2.0 * jnp.tanh((sums - mean) / 2.0)
        return mine, lax.ppermute(mine, "pair", mates)

    capped = [capped_of(unit) for unit in units]

    sizes = (across, rows, pairs)
    operator = None
    early = units[:-final]
    for first in range(0, len(early), 2):
        group = range(first, min(first + 2, len(early)))
        operator = accumulate(
            [capped[u][0] for u in group],
            [capped[u][1] for u in group],
            noise,
            [part for u in group for _, part in units[u]],
            [piece for u in group for piece, _ in units[u]],
            mine_scalars,
            operator,
            sizes,
        )
    late = range(len(early), len(units))
    stack = stack_of([part for u in late for _, part in units[u]])
    late_pieces = [piece for u in late for piece, _ in units[u]]
    scale = math.sqrt(total_pairs / fields)
    block = rows // 2 if rows % 256 == 0 else rows
    one_body = finish(
        [capped[u][0] for u in late], noise, stack, operator, late_pieces, mine_scalars, scale, None, block
    )
    one_body = finish(
        [capped[u][1] for u in late], noise, stack, operator, late_pieces, other_scalars, scale, one_body, block
    )

    share = jnp.zeros((channels, fields, rows), jnp.float32)
    for unit, (mine, _) in zip(units, capped):
        own = lax.dynamic_index_in_dim(mine, chip, 1, keepdims=False)
        at = 0
        for (step, start, n, _), _ in unit:
            part = own[:, at : at + n]
            share = lax.dynamic_update_slice_in_dim(share, part, owners[step] * shard + start, axis=1)
            at += n
    return (share.transpose(0, 2, 1), one_body.reshape(walkers, channels, pairs))


def solution(mesh):
    return jax.shard_map(
        functools.partial(per_device, mesh.shape["field"], mesh.shape["pair"]),
        mesh=mesh,
        in_specs=(
            P(("grp", "field"), "pair"),
            P(None, ("grp", "field"), "pair"),
            P(None, "grp"),
            P(("grp", "field"), None),
        ),
        out_specs=(P(None, ("grp", "field", "pair"), None), P(("grp", "field"), None, "pair")),
        check_vma=False,
    )
```

```python
import functools
import math

import jax
import jax.numpy as jnp
from jax import lax
from jax.experimental import pallas as pl
from jax.experimental.pallas import tpu as pltpu
from jax.sharding import PartitionSpec as P

CORES = 2
MIB = 1024 * 1024
ROWS_DOT = (((1,), (1,)), ((), ()))
DOT = (((1,), (0,)), ((), ()))
WHOLE = pl.BlockSpec(memory_space=pltpu.VMEM)
COST = pl.CostEstimate(flops=1, bytes_accessed=1, transcendentals=0)


def split(x):
    high = x.astype(jnp.bfloat16)
    return high, (x - high.astype(jnp.float32)).astype(jnp.bfloat16)


def params(mib):
    return pltpu.CompilerParams(vmem_limit_bytes=mib * MIB)


def stacked(parts):
    return parts[0] if len(parts) == 1 else jnp.concatenate(parts, 0)


def split_green_kernel(s_ref, green_ref, own_high_ref, own_low_ref, mate_high_ref, mate_low_ref):
    at = (pl.program_id(0), pl.program_id(1))
    high, low = split(green_ref[0, 0, 0])
    own = pl.program_id(2) == s_ref[0]

    @pl.when(own)
    def _():
        own_high_ref[at], own_low_ref[at] = high, low

    @pl.when(jnp.logical_not(own))
    def _():
        mate_high_ref[at], mate_low_ref[at] = high, low


def split_green(scalars, green):
    channels, across, cores, rows, pairs = green.shape
    return pl.pallas_call(
        split_green_kernel,
        out_shape=[pltpu.VMEM((channels, across, rows, pairs), jnp.bfloat16)] * 4,
        grid=(channels, across, cores),
        in_specs=[
            pl.BlockSpec(memory_space=pltpu.SMEM),
            pl.BlockSpec((1, 1, 1, rows, pairs), lambda c, x, h: (c, x, h, 0, 0)),
        ],
        out_specs=[WHOLE] * 4,
        compiler_params=params(12),
        cost_estimate=COST,
        name="split_green",
    )(scalars, green)


def bias_kernel(n, high_ref, low_ref, *refs):
    parts, out_refs, chol = refs[:n], refs[n:-1], refs[-1]
    fields = chol.shape[0] // 2
    chol[:fields], chol[fields:] = split(stacked([part[...] for part in parts]))
    channels, across = high_ref.shape[:2]
    for c in range(channels):
        for x in range(across):
            both = lax.dot_general(chol[...], high_ref[c, x], ROWS_DOT, preferred_element_type=jnp.float32)
            cross = lax.dot_general(chol[:fields], low_ref[c, x], ROWS_DOT, preferred_element_type=jnp.float32)
            out_refs[c][x] = both[:fields] + (both[fields:] + cross)


def bias_of(high, low, parts):
    channels, across, rows, pairs = high.shape
    fields = sum(part.shape[0] for part in parts)
    return pl.pallas_call(
        functools.partial(bias_kernel, len(parts)),
        out_shape=[jax.ShapeDtypeStruct((across, fields, rows), jnp.float32)] * channels,
        in_specs=[WHOLE] * (2 + len(parts)),
        out_specs=[WHOLE] * channels,
        scratch_shapes=[pltpu.VMEM((2 * fields, pairs), jnp.bfloat16)],
        compiler_params=params(10),
        cost_estimate=COST,
        name="bias",
    )(high, low, *parts)


def add_kernel(n, *refs):
    for c in range(n):
        refs[-1][c] = refs[c][...] + refs[n + c][...]


def add(a, b):
    return pl.pallas_call(
        functools.partial(add_kernel, len(a)),
        out_shape=jax.ShapeDtypeStruct((len(a), *a[0].shape), a[0].dtype),
        in_specs=[WHOLE] * (2 * len(a)),
        out_specs=WHOLE,
        compiler_params=params(6),
        cost_estimate=COST,
        name="add",
    )(*a, *b)


def cap_kernel(unit, s_ref, mean_ref, sums_ref, more_ref, *refs):
    channels, across, fields, _ = sums_ref.shape
    capped_refs, share_ref = refs[-1 - channels : -1], refs[-1]
    means = [mean_ref[s_ref[2 + step], start : start + rows] for step, start, rows, _ in unit]
    for c in range(channels):
        mean = stacked([column[:, c : c + 1] for column in means])
        for x in range(across):
            capped_refs[c][x] = 2.0 * jnp.tanh((sums_ref[c, x] + more_ref[c, x] - mean) / 2.0)
        at = 0
        for step, start, rows, shard in unit:
            to = pl.ds(pl.multiple_of(s_ref[2 + step] * shard + start, 8), rows)
            share_ref[c, to, :] = capped_refs[c][s_ref[1], at : at + rows]
            at += rows


def cap(unit, scalars, means, sums, more, share, all_fields):
    channels, _, _, rows = sums.shape
    operands = [scalars, means, sums, more]
    in_specs = [pl.BlockSpec(memory_space=pltpu.SMEM), WHOLE, WHOLE, WHOLE]
    aliases = {}
    if share is not None:
        aliases = {len(operands): channels}
        operands.append(share)
        in_specs.append(WHOLE)
    return pl.pallas_call(
        functools.partial(cap_kernel, unit),
        out_shape=[jax.ShapeDtypeStruct(sums.shape[1:], jnp.float32)] * channels
        + [pltpu.VMEM((channels, all_fields, rows), jnp.float32)],
        in_specs=in_specs,
        out_specs=[WHOLE] * (channels + 1),
        input_output_aliases=aliases,
        compiler_params=params(8),
        cost_estimate=COST,
        name="cap",
    )(*operands)


def stack_chol(out, parts):
    high, low = split(stacked([part[...] for part in parts]))
    depth = high.shape[0]
    out[:depth] = high
    out[depth : 2 * depth] = high
    out[2 * depth :] = low


def stack_fields(capped, noise):
    first = stacked(noise) - stacked(capped[0::2])
    second = -stacked(capped[1::2])
    high, low = split(jnp.concatenate([first, second], 1))
    return jnp.concatenate([high, low, high], 0).T


def noise_specs(unit, noise, lanes, rows):
    apart, blocks = noise.shape[1] > 1, rows // lanes

    def spec(step, shard):
        def at(x, h, b, s):
            share = x * CORES + h
            return (s[2 + step], share, 0, b) if apart else (s[2 + step], 0, 0, share * blocks + b)

        return pl.BlockSpec((1, 1, shard, lanes), at)

    return [spec(step, shard) for step, _, _, shard in unit]


def noise_pieces(refs, unit):
    return [ref[0, 0, start : start + rows] for ref, (_, start, rows, _) in zip(refs, unit)]


def stack_kernel(*refs):
    stack_chol(refs[-1], refs[:-1])


def stack_of(chol):
    depth = sum(part.shape[0] for part in chol)
    return pl.pallas_call(
        stack_kernel,
        out_shape=pltpu.VMEM((3 * depth, chol[0].shape[1]), jnp.bfloat16),
        in_specs=[WHOLE] * len(chol),
        out_specs=WHOLE,
        compiler_params=params(12),
        cost_estimate=COST,
        name="stack_cholesky",
    )(*chol)


def finish_kernel(n, m, unit, scale, with_share, s_ref, *refs):
    capped, noise, stack = refs[:n], refs[n : n + m], refs[n + m]
    left = refs[-1]
    out_ref = refs[-3] if with_share else refs[-2]
    x, p = pl.program_id(0), pl.program_id(1)

    if with_share:

        @pl.when((x == 0) & (p == 0))
        def _():
            for c in range(2):
                refs[-2][c] = refs[-4][c].T

    @pl.when(p == 0)
    def _():
        left[...] = stack_fields([part[0] for part in capped], noise_pieces(noise, unit))

    width = out_ref.shape[-1]
    columns = pl.ds(pl.multiple_of(p * width, 128), width)
    sums = scale * lax.dot_general(left[...], stack[:, columns], DOT, preferred_element_type=jnp.float32)
    rows = sums.shape[0] // 2
    for c in range(2):
        out_ref[0, 0, :, c, :] = sums[c * rows : (c + 1) * rows]


def finish(capped, noise, stack, unit, scalars, scale, earlier, share, sizes):
    across, rows, pairs = sizes
    tiles = 3 if pairs % 384 == 0 else 1
    in_specs = [pl.BlockSpec((1, *part.shape[1:]), lambda x, p, s: (x, 0, 0)) for part in capped]
    in_specs += [
        pl.BlockSpec(spec.block_shape, lambda x, p, s, at=spec.index_map: at(x, s[0], 0, s))
        for spec in noise_specs(unit, noise, rows, rows)
    ]
    in_specs += [WHOLE]
    operands = [scalars, *capped, *([noise] * len(unit)), stack]
    aliases = {}
    if earlier is not None:
        in_specs.append(pl.BlockSpec(memory_space=pl.ANY))
        aliases = {len(operands): 0}
        operands.append(earlier)
    out_shape = [jax.ShapeDtypeStruct((across, CORES, rows, 2, pairs), jnp.float32)]
    out_specs = [pl.BlockSpec((1, 1, rows, 2, pairs // tiles), lambda x, p, s: (x, s[0], 0, 0, p))]
    if share is not None:
        turned = (share.shape[0], share.shape[2], share.shape[1])
        out_shape.append(jax.ShapeDtypeStruct(turned, jnp.float32))
        out_specs.append(pl.BlockSpec(turned, lambda x, p, s: (0, 0, 0)))
        in_specs.append(WHOLE)
        operands.append(share)
    return pl.pallas_call(
        functools.partial(finish_kernel, len(capped), len(unit), unit, scale, share is not None),
        out_shape=out_shape,
        grid_spec=pltpu.PrefetchScalarGridSpec(
            num_scalar_prefetch=1,
            grid=(across, tiles),
            in_specs=in_specs,
            out_specs=out_specs,
            scratch_shapes=[pltpu.VMEM((2 * rows, stack.shape[0]), jnp.bfloat16)],
        ),
        input_output_aliases=aliases,
        compiler_params=params(36),
        cost_estimate=COST,
        name="finish",
    )(*operands)


def after(x, *earlier):
    return lax.optimization_barrier((x, *earlier))[0]


def per_device(ring_size, pair_size, cholesky_tensor, green_function, mean_field, field_noise):
    shard, pairs = cholesky_tensor.shape
    channels, walkers, _ = green_function.shape
    fields = ring_size * shard
    total_pairs = pair_size * pairs
    across = pair_size // CORES
    rows = walkers // pair_size
    sizes = (across, rows, pairs)
    scale = math.sqrt(total_pairs / fields)

    place, member = lax.axis_index("field"), lax.axis_index("pair")
    core, chip = member % CORES, member // CORES
    owners = [(place - step) % ring_size for step in range(ring_size)]
    own_scalars = jnp.stack([core, chip, *owners]).astype(jnp.int32)
    mate_scalars = jnp.stack([1 - core, chip, *owners]).astype(jnp.int32)

    ring = [(i, (i + 1) % ring_size) for i in range(ring_size)]
    mates = [(i, i ^ 1) for i in range(pair_size)]

    count = 2 if shard % 32 == 0 and ring_size > 2 else 1
    cuts = [(i * (shard // count), shard // count) for i in range(count)]
    pieces = [(step, start, n, shard) for step in range(1, ring_size) for start, n in cuts]
    held = {(0, start): lax.slice_in_dim(cholesky_tensor, start, start + n, axis=0) for start, n in cuts}

    own_piece = (0, 0, shard, shard)
    if count > 1:
        units = [[own_piece]] + [pieces[i : i + 2] for i in range(0, len(pieces) - 2, 2)] + [[p] for p in pieces[-2:]]
    else:
        run = 1
        while run * shard % 16 or run * 8 < ring_size:
            run *= 2
        line = [own_piece, *pieces]
        units = [line[i : i + run] for i in range(0, len(line), run)]
    n_units = len(units)

    def hop(step, start, token):
        held[step, start] = lax.ppermute(after(held[step - 1, start], *token), "field", ring)

    def parts_of(unit):
        return [cholesky_tensor if piece == own_piece else held[piece[0], piece[1]] for piece in unit]

    for start, _ in cuts:
        hop(1, start, ())
    green = green_function.reshape(channels, across, CORES, rows, pairs)
    turned = field_noise.T
    if rows % 128:
        noise = turned.reshape(ring_size, shard, pair_size, rows).transpose(0, 2, 1, 3)
    else:
        noise = turned.reshape(ring_size, 1, shard, walkers)
    means = mean_field.T.reshape(ring_size, shard, channels)
    ready = [held[0, start] for start, _ in cuts] + [noise, means, mate_scalars]
    own_high, own_low, mate_high, mate_low = split_green(after(own_scalars, *ready), green)
    state = {"share": None, "token": ()}
    fronts, sums, own, mate = {}, {}, {}, {}

    def front(u):
        parts = parts_of(units[u])
        parts[0] = after(parts[0], *state["token"])
        sent = bias_of(mate_high, mate_low, parts)
        arrived = [lax.ppermute(part, "pair", mates) for part in sent]
        kept = bias_of(own_high, own_low, [after(parts[0], *sent), *parts[1:]])
        state["token"] = tuple(kept)
        fronts[u] = (kept, arrived)

    def across_chips(u):
        kept, arrived = fronts[u]
        total = add(kept, arrived)
        reach = CORES
        while 2 * reach < pair_size:
            more = lax.ppermute(total, "pair", [(i, i ^ reach) for i in range(pair_size)])
            total = add([total[c] for c in range(channels)], [more[c] for c in range(channels)])
            reach *= 2
        sums[u] = (total, lax.ppermute(total, "pair", [(i, i ^ reach) for i in range(pair_size)]))

    def back(u):
        total, more = sums[u]
        *own[u], state["share"] = cap(
            units[u], own_scalars, means, total, more, state["share"], fields
        )
        mate[u] = [lax.ppermute(part, "pair", mates) for part in own[u]]

    def send_on(piece):
        step, start, _, _ = piece
        arrived = held[step, start]
        if step + 1 < ring_size:
            hop(step + 1, start, state["token"])
        state["token"] = (*state["token"], arrived)

    if count > 1:
        front(0)
        across_chips(0)
        for step in range(1, ring_size):
            send_on(pieces[2 * step - 2])
            if step + 1 == ring_size:
                front(n_units - 2)
            state["token"] += (sums[step - 1][0],) + ((own[step - 2][0],) if step > 1 else ())
            send_on(pieces[2 * step - 1])
            if step + 1 < ring_size:
                front(step)
                across_chips(step)
                back(step - 1)
        across_chips(n_units - 2)
        state["token"] += (sums[n_units - 2][0],)
        front(n_units - 1)
        across_chips(n_units - 1)
        state["token"] += (sums[n_units - 1][0],)
    else:
        for u, unit in enumerate(units):
            for piece in unit:
                if piece != own_piece:
                    send_on(piece)
            front(u)
            across_chips(u)
    for u in range(n_units):
        if u not in own:
            back(u)
    line = [piece for unit in units for piece in unit]
    parts = [part for unit in units for part in parts_of(unit)]
    stack = stack_of([after(parts[0], *state["token"]), *parts[1:]])
    (one_body,) = finish(
        [part for u in range(n_units) for part in own[u]], noise, stack, line, own_scalars, scale, None, None, sizes
    )
    one_body, capped = finish(
        [part for u in range(n_units) for part in mate[u]], noise, stack, line, mate_scalars, scale, one_body,
        state["share"], sizes,
    )
    return (capped, one_body.reshape(walkers, channels, pairs))


def solution(mesh):
    return jax.shard_map(
        functools.partial(per_device, mesh.shape["field"], mesh.shape["pair"]),
        mesh=mesh,
        in_specs=(
            P(("grp", "field"), "pair"),
            P(None, ("grp", "field"), "pair"),
            P(None, "grp"),
            P(("grp", "field"), None),
        ),
        out_specs=(P(None, ("grp", "field", "pair"), None), P(("grp", "field"), None, "pair")),
        check_vma=False,
    )
```

```python
import functools
import math

import jax
import jax.numpy as jnp
from jax import lax
from jax.experimental import pallas as pl
from jax.experimental.pallas import tpu as pltpu
from jax.sharding import PartitionSpec as P

CORES = 2
MIB = 1024 * 1024
ROWS_DOT = (((1,), (1,)), ((), ()))
DOT = (((1,), (0,)), ((), ()))
WHOLE = pl.BlockSpec(memory_space=pltpu.VMEM)
COST = pl.CostEstimate(flops=1, bytes_accessed=1, transcendentals=0)


def split(x):
    high = x.astype(jnp.bfloat16)
    return high, (x - high.astype(jnp.float32)).astype(jnp.bfloat16)


def params(mib):
    return pltpu.CompilerParams(vmem_limit_bytes=mib * MIB)


def stacked(parts):
    return parts[0] if len(parts) == 1 else jnp.concatenate(parts, 0)


def split_green_kernel(s_ref, green_ref, own_high_ref, own_low_ref, mate_high_ref, mate_low_ref):
    at = (pl.program_id(0), pl.program_id(1))
    high, low = split(green_ref[0, 0, 0])
    own = pl.program_id(2) == s_ref[0]

    @pl.when(own)
    def _():
        own_high_ref[at], own_low_ref[at] = high, low

    @pl.when(jnp.logical_not(own))
    def _():
        mate_high_ref[at], mate_low_ref[at] = high, low


def split_green(scalars, green):
    channels, across, cores, rows, pairs = green.shape
    return pl.pallas_call(
        split_green_kernel,
        out_shape=[pltpu.VMEM((channels, across, rows, pairs), jnp.bfloat16)] * 4,
        grid=(channels, across, cores),
        in_specs=[
            pl.BlockSpec(memory_space=pltpu.SMEM),
            pl.BlockSpec((1, 1, 1, rows, pairs), lambda c, x, h: (c, x, h, 0, 0)),
        ],
        out_specs=[WHOLE] * 4,
        compiler_params=params(12),
        cost_estimate=COST,
        name="split_green",
    )(scalars, green)


def bias_kernel(n, high_ref, low_ref, *refs):
    parts, out_refs, chol = refs[:n], refs[n:-1], refs[-1]
    fields = chol.shape[0] // 2
    chol[:fields], chol[fields:] = split(stacked([part[...] for part in parts]))
    channels, across = high_ref.shape[:2]
    for c in range(channels):
        for x in range(across):
            both = lax.dot_general(chol[...], high_ref[c, x], ROWS_DOT, preferred_element_type=jnp.float32)
            cross = lax.dot_general(chol[:fields], low_ref[c, x], ROWS_DOT, preferred_element_type=jnp.float32)
            out_refs[c][x] = both[:fields] + (both[fields:] + cross)


def bias_of(high, low, parts):
    channels, across, rows, pairs = high.shape
    fields = sum(part.shape[0] for part in parts)
    return pl.pallas_call(
        functools.partial(bias_kernel, len(parts)),
        out_shape=[jax.ShapeDtypeStruct((across, fields, rows), jnp.float32)] * channels,
        in_specs=[WHOLE] * (2 + len(parts)),
        out_specs=[WHOLE] * channels,
        scratch_shapes=[pltpu.VMEM((2 * fields, pairs), jnp.bfloat16)],
        compiler_params=params(10),
        cost_estimate=COST,
        name="bias",
    )(high, low, *parts)


def add_kernel(n, *refs):
    for c in range(n):
        refs[-1][c] = refs[c][...] + refs[n + c][...]


def add(a, b):
    return pl.pallas_call(
        functools.partial(add_kernel, len(a)),
        out_shape=jax.ShapeDtypeStruct((len(a), *a[0].shape), a[0].dtype),
        in_specs=[WHOLE] * (2 * len(a)),
        out_specs=WHOLE,
        compiler_params=params(6),
        cost_estimate=COST,
        name="add",
    )(*a, *b)


def cap_kernel(unit, s_ref, mean_ref, sums_ref, more_ref, *refs):
    channels, across, fields, _ = sums_ref.shape
    capped_refs, share_ref = refs[-1 - channels : -1], refs[-1]
    means = [mean_ref[s_ref[2 + step], start : start + rows] for step, start, rows, _ in unit]
    for c in range(channels):
        mean = stacked([column[:, c : c + 1] for column in means])
        for x in range(across):
            capped_refs[c][x] = 2.0 * jnp.tanh((sums_ref[c, x] + more_ref[c, x] - mean) / 2.0)
        at = 0
        for step, start, rows, shard in unit:
            to = pl.ds(pl.multiple_of(s_ref[2 + step] * shard + start, 8), rows)
            share_ref[c, to, :] = capped_refs[c][s_ref[1], at : at + rows]
            at += rows


def cap(unit, scalars, means, sums, more, share, all_fields):
    channels, _, _, rows = sums.shape
    operands = [scalars, means, sums, more]
    in_specs = [pl.BlockSpec(memory_space=pltpu.SMEM), WHOLE, WHOLE, WHOLE]
    aliases = {}
    if share is not None:
        aliases = {len(operands): channels}
        operands.append(share)
        in_specs.append(WHOLE)
    return pl.pallas_call(
        functools.partial(cap_kernel, unit),
        out_shape=[jax.ShapeDtypeStruct(sums.shape[1:], jnp.float32)] * channels
        + [pltpu.VMEM((channels, all_fields, rows), jnp.float32)],
        in_specs=in_specs,
        out_specs=[WHOLE] * (channels + 1),
        input_output_aliases=aliases,
        compiler_params=params(8),
        cost_estimate=COST,
        name="cap",
    )(*operands)


def stack_chol(out, parts):
    high, low = split(stacked([part[...] for part in parts]))
    depth = high.shape[0]
    out[:depth] = high
    out[depth : 2 * depth] = high
    out[2 * depth :] = low


def stack_fields(capped, noise):
    first = stacked(noise) - stacked(capped[0::2])
    second = -stacked(capped[1::2])
    high, low = split(jnp.concatenate([first, second], 1))
    return jnp.concatenate([high, low, high], 0).T


def noise_specs(unit, noise, lanes, rows):
    apart, blocks = noise.shape[1] > 1, rows // lanes

    def spec(step, shard):
        def at(x, h, b, s):
            share = x * CORES + h
            return (s[2 + step], share, 0, b) if apart else (s[2 + step], 0, 0, share * blocks + b)

        return pl.BlockSpec((1, 1, shard, lanes), at)

    return [spec(step, shard) for step, _, _, shard in unit]


def noise_pieces(refs, unit):
    return [ref[0, 0, start : start + rows] for ref, (_, start, rows, _) in zip(refs, unit)]


def stack_kernel(*refs):
    stack_chol(refs[-1], refs[:-1])


def stack_of(chol):
    depth = sum(part.shape[0] for part in chol)
    return pl.pallas_call(
        stack_kernel,
        out_shape=pltpu.VMEM((3 * depth, chol[0].shape[1]), jnp.bfloat16),
        in_specs=[WHOLE] * len(chol),
        out_specs=WHOLE,
        compiler_params=params(12),
        cost_estimate=COST,
        name="stack_cholesky",
    )(*chol)


def begin_kernel(n, unit, s_ref, *refs):
    mine, other, noise, (stack, out_ref) = refs[:n], refs[n : 2 * n], refs[2 * n : -2], refs[-2:]
    x, core = pl.program_id(0), pl.program_id(1)
    own = core == s_ref[0]
    capped = [jnp.where(own, a[0], b[0]) for a, b in zip(mine, other)]
    out_ref[x, core] = lax.dot_general(
        stack_fields(capped, noise_pieces(noise, unit)), stack[...], DOT, preferred_element_type=jnp.float32
    )


def begin(mine, other, noise, stack, unit, scalars, sizes):
    across, rows, pairs = sizes
    in_specs = [pl.BlockSpec((1, *part.shape[1:]), lambda x, h, s: (x, 0, 0)) for part in (*mine, *other)]
    in_specs += [
        pl.BlockSpec(spec.block_shape, lambda x, h, s, at=spec.index_map: at(x, h, 0, s))
        for spec in noise_specs(unit, noise, rows, rows)
    ]
    return pl.pallas_call(
        functools.partial(begin_kernel, len(mine), unit),
        out_shape=pltpu.VMEM((across, CORES, 2 * rows, pairs), jnp.float32),
        grid_spec=pltpu.PrefetchScalarGridSpec(
            num_scalar_prefetch=1, grid=(across, CORES), in_specs=[*in_specs, WHOLE], out_specs=WHOLE
        ),
        compiler_params=params(16),
        cost_estimate=COST,
        name="begin",
    )(scalars, *mine, *other, *([noise] * len(unit)), stack)


def finish_kernel(n, m, unit, scale, s_ref, *refs):
    mine, other, noise = refs[:n], refs[n : 2 * n], refs[2 * n : 2 * n + m]
    stack, prior, share, out_ref, turned_ref, left = refs[2 * n + m :]
    turn, x, p = pl.program_id(0), pl.program_id(1), pl.program_id(2)
    core = (s_ref[0] + turn) % CORES

    @pl.when((turn == 0) & (x == 0) & (p == 0))
    def _():
        for c in range(2):
            turned_ref[c] = share[c].T

    @pl.when(p == 0)
    def _():
        capped = [jnp.where(turn == 0, a[0], b[0]) for a, b in zip(mine, other)]
        left[...] = stack_fields(capped, noise_pieces(noise, unit))

    width = out_ref.shape[-1]
    columns = pl.ds(pl.multiple_of(p * width, 128), width)
    sums = lax.dot_general(left[...], stack[:, columns], DOT, preferred_element_type=jnp.float32)
    rows = sums.shape[0] // 2
    for c in range(2):
        part = slice(c * rows, (c + 1) * rows)
        out_ref[0, 0, :, c, :] = scale * (prior[x, core, part, columns] + sums[part])


def finish(mine, other, noise, stack, prior, share, unit, scalars, scale, sizes):
    across, rows, pairs = sizes
    tiles = 3 if pairs % 384 == 0 else 1
    turned = (share.shape[0], share.shape[2], share.shape[1])
    in_specs = [pl.BlockSpec((1, *part.shape[1:]), lambda t, x, p, s: (x, 0, 0)) for part in (*mine, *other)]
    in_specs += [
        pl.BlockSpec(spec.block_shape, lambda t, x, p, s, at=spec.index_map: at(x, (s[0] + t) % CORES, 0, s))
        for spec in noise_specs(unit, noise, rows, rows)
    ]
    return pl.pallas_call(
        functools.partial(finish_kernel, len(mine), len(unit), unit, scale),
        out_shape=[
            jax.ShapeDtypeStruct((across, CORES, rows, 2, pairs), jnp.float32),
            jax.ShapeDtypeStruct(turned, jnp.float32),
        ],
        grid_spec=pltpu.PrefetchScalarGridSpec(
            num_scalar_prefetch=1,
            grid=(CORES, across, tiles),
            in_specs=[*in_specs, WHOLE, WHOLE, WHOLE],
            out_specs=[
                pl.BlockSpec(
                    (1, 1, rows, 2, pairs // tiles), lambda t, x, p, s: (x, (s[0] + t) % CORES, 0, 0, p)
                ),
                pl.BlockSpec(turned, lambda t, x, p, s: (0, 0, 0)),
            ],
            scratch_shapes=[pltpu.VMEM((2 * rows, stack.shape[0]), jnp.bfloat16)],
        ),
        compiler_params=params(16),
        cost_estimate=COST,
        name="finish",
    )(scalars, *mine, *other, *([noise] * len(unit)), stack, prior, share)


def after(x, *earlier):
    return lax.optimization_barrier((x, *earlier))[0]


def per_device(ring_size, pair_size, cholesky_tensor, green_function, mean_field, field_noise):
    shard, pairs = cholesky_tensor.shape
    channels, walkers, _ = green_function.shape
    fields = ring_size * shard
    total_pairs = pair_size * pairs
    across = pair_size // CORES
    rows = walkers // pair_size
    sizes = (across, rows, pairs)
    scale = math.sqrt(total_pairs / fields)

    place, member = lax.axis_index("field"), lax.axis_index("pair")
    core, chip = member % CORES, member // CORES
    owners = [(place - step) % ring_size for step in range(ring_size)]
    own_scalars = jnp.stack([core, chip, *owners]).astype(jnp.int32)
    mate_scalars = jnp.stack([1 - core, chip, *owners]).astype(jnp.int32)

    ring = [(i, (i + 1) % ring_size) for i in range(ring_size)]
    mates = [(i, i ^ 1) for i in range(pair_size)]

    count = 2 if shard % 32 == 0 and ring_size > 2 else 1
    cuts = [(i * (shard // count), shard // count) for i in range(count)]
    pieces = [(step, start, n, shard) for step in range(1, ring_size) for start, n in cuts]
    held = {(0, start): lax.slice_in_dim(cholesky_tensor, start, start + n, axis=0) for start, n in cuts}

    own_piece = (0, 0, shard, shard)
    if count > 1:
        units = [[own_piece]] + [pieces[i : i + 2] for i in range(0, len(pieces) - 2, 2)] + [[p] for p in pieces[-2:]]
    else:
        run = 1
        while run * shard % 16 or run * 8 < ring_size:
            run *= 2
        line = [own_piece, *pieces]
        units = [line[i : i + run] for i in range(0, len(line), run)]
    n_units = len(units)

    def hop(step, start, token):
        held[step, start] = lax.ppermute(after(held[step - 1, start], *token), "field", ring)

    def parts_of(unit):
        return [cholesky_tensor if piece == own_piece else held[piece[0], piece[1]] for piece in unit]

    for start, _ in cuts:
        hop(1, start, ())
    green = green_function.reshape(channels, across, CORES, rows, pairs)
    turned = field_noise.T
    if rows % 128:
        noise = turned.reshape(ring_size, shard, pair_size, rows).transpose(0, 2, 1, 3)
    else:
        noise = turned.reshape(ring_size, 1, shard, walkers)
    means = mean_field.T.reshape(ring_size, shard, channels)
    ready = [held[0, start] for start, _ in cuts] + [noise, means, mate_scalars]
    own_high, own_low, mate_high, mate_low = split_green(after(own_scalars, *ready), green)
    state = {"share": None, "token": ()}
    fronts, sums, own, mate = {}, {}, {}, {}

    def front(u):
        parts = parts_of(units[u])
        parts[0] = after(parts[0], *state["token"])
        sent = bias_of(mate_high, mate_low, parts)
        arrived = [lax.ppermute(part, "pair", mates) for part in sent]
        kept = bias_of(own_high, own_low, [after(parts[0], *sent), *parts[1:]])
        state["token"] = tuple(kept)
        fronts[u] = (kept, arrived)

    def across_chips(u):
        kept, arrived = fronts[u]
        total = add(kept, arrived)
        reach = CORES
        while 2 * reach < pair_size:
            more = lax.ppermute(total, "pair", [(i, i ^ reach) for i in range(pair_size)])
            total = add([total[c] for c in range(channels)], [more[c] for c in range(channels)])
            reach *= 2
        sums[u] = (total, lax.ppermute(total, "pair", [(i, i ^ reach) for i in range(pair_size)]))

    def back(u, tie=()):
        total, more = sums[u]
        *own[u], state["share"] = cap(
            units[u], own_scalars, after(means, *tie), total, more, state["share"], fields
        )
        mate[u] = [lax.ppermute(part, "pair", mates) for part in own[u]]

    def send_on(piece):
        step, start, _, _ = piece
        arrived = held[step, start]
        if step + 1 < ring_size:
            hop(step + 1, start, state["token"])
        state["token"] = (*state["token"], arrived)

    if count > 1:
        front(0)
        across_chips(0)
        for step in range(1, ring_size):
            send_on(pieces[2 * step - 2])
            if step + 1 == ring_size:
                front(n_units - 2)
            state["token"] += (sums[step - 1][0],) + ((own[step - 2][0],) if step > 1 else ())
            send_on(pieces[2 * step - 1])
            if step + 1 < ring_size:
                front(step)
                across_chips(step)
                back(step - 1)
        across_chips(n_units - 2)
        state["token"] += (sums[n_units - 2][0],)
        front(n_units - 1)
        across_chips(n_units - 1)
        state["token"] += (sums[n_units - 1][0],)
        final = 3
    else:
        for u, unit in enumerate(units):
            for piece in unit:
                if piece != own_piece:
                    send_on(piece)
            front(u)
            across_chips(u)
            if u:
                back(u - 1)
        state["token"] += (sums[n_units - 1][0],)
        final = 1

    def stack_and_pieces(chosen):
        parts = [part for u in chosen for part in parts_of(units[u])]
        return stack_of([after(parts[0], *state["token"]), *parts[1:]]), [piece for u in chosen for piece in units[u]]

    def channels_of(capped, chosen):
        return [part for u in chosen for part in capped[u]]

    first, late = range(n_units - final), range(n_units - final, n_units)
    stack, line = stack_and_pieces(first)
    operator = begin(channels_of(own, first), channels_of(mate, first), noise, stack, line, own_scalars, sizes)
    stack, line = stack_and_pieces(late)
    for u in late:
        if u not in own:
            back(u, (operator, stack))
    one_body, capped = finish(
        channels_of(own, late), channels_of(mate, late), noise, stack, operator, state["share"], line, own_scalars,
        scale, sizes,
    )
    return (capped, one_body.reshape(walkers, channels, pairs))


def solution(mesh):
    return jax.shard_map(
        functools.partial(per_device, mesh.shape["field"], mesh.shape["pair"]),
        mesh=mesh,
        in_specs=(
            P(("grp", "field"), "pair"),
            P(None, ("grp", "field"), "pair"),
            P(None, "grp"),
            P(("grp", "field"), None),
        ),
        out_specs=(P(None, ("grp", "field", "pair"), None), P(("grp", "field"), None, "pair")),
        check_vma=False,
    )
```

```python
import functools
import math

import jax
import jax.numpy as jnp
from jax import lax
from jax.experimental import pallas as pl
from jax.experimental.pallas import tpu as pltpu
from jax.sharding import PartitionSpec as P

CORES = 2
MIB = 1024 * 1024
ROWS_DOT = (((1,), (1,)), ((), ()))
DOT = (((1,), (0,)), ((), ()))
WHOLE = pl.BlockSpec(memory_space=pltpu.VMEM)
COST = pl.CostEstimate(flops=1, bytes_accessed=1, transcendentals=0)


def split(x):
    high = x.astype(jnp.bfloat16)
    return high, (x - high.astype(jnp.float32)).astype(jnp.bfloat16)


def params(mib):
    return pltpu.CompilerParams(vmem_limit_bytes=mib * MIB)


def stacked(parts):
    return parts[0] if len(parts) == 1 else jnp.concatenate(parts, 0)


def split_green_kernel(s_ref, green_ref, own_high_ref, own_low_ref, mate_high_ref, mate_low_ref):
    at = (pl.program_id(0), pl.program_id(1))
    high, low = split(green_ref[0, 0, 0])
    own = pl.program_id(2) == s_ref[0]

    @pl.when(own)
    def _():
        own_high_ref[at], own_low_ref[at] = high, low

    @pl.when(jnp.logical_not(own))
    def _():
        mate_high_ref[at], mate_low_ref[at] = high, low


def split_green(scalars, green):
    channels, across, cores, rows, pairs = green.shape
    return pl.pallas_call(
        split_green_kernel,
        out_shape=[pltpu.VMEM((channels, across, rows, pairs), jnp.bfloat16)] * 4,
        grid=(channels, across, cores),
        in_specs=[
            pl.BlockSpec(memory_space=pltpu.SMEM),
            pl.BlockSpec((1, 1, 1, rows, pairs), lambda c, x, h: (c, x, h, 0, 0)),
        ],
        out_specs=[WHOLE] * 4,
        compiler_params=params(12),
        cost_estimate=COST,
        name="split_green",
    )(scalars, green)


def bias_kernel(n, high_ref, low_ref, *refs):
    parts, out_refs, chol = refs[:n], refs[n:-1], refs[-1]
    fields = chol.shape[0] // 2
    chol[:fields], chol[fields:] = split(stacked([part[...] for part in parts]))
    channels, across = high_ref.shape[:2]
    for c in range(channels):
        for x in range(across):
            both = lax.dot_general(chol[...], high_ref[c, x], ROWS_DOT, preferred_element_type=jnp.float32)
            cross = lax.dot_general(chol[:fields], low_ref[c, x], ROWS_DOT, preferred_element_type=jnp.float32)
            out_refs[c][x] = both[:fields] + (both[fields:] + cross)


def bias_of(high, low, parts):
    channels, across, rows, pairs = high.shape
    fields = sum(part.shape[0] for part in parts)
    return pl.pallas_call(
        functools.partial(bias_kernel, len(parts)),
        out_shape=[jax.ShapeDtypeStruct((across, fields, rows), jnp.float32)] * channels,
        in_specs=[WHOLE] * (2 + len(parts)),
        out_specs=[WHOLE] * channels,
        scratch_shapes=[pltpu.VMEM((2 * fields, pairs), jnp.bfloat16)],
        compiler_params=params(10),
        cost_estimate=COST,
        name="bias",
    )(high, low, *parts)


def add_kernel(n, *refs):
    for c in range(n):
        refs[-1][c] = refs[c][...] + refs[n + c][...]


def add(a, b):
    return pl.pallas_call(
        functools.partial(add_kernel, len(a)),
        out_shape=jax.ShapeDtypeStruct((len(a), *a[0].shape), a[0].dtype),
        in_specs=[WHOLE] * (2 * len(a)),
        out_specs=WHOLE,
        compiler_params=params(6),
        cost_estimate=COST,
        name="add",
    )(*a, *b)


def cap_kernel(unit, s_ref, mean_ref, sums_ref, more_ref, *refs):
    channels, across, fields, _ = sums_ref.shape
    capped_refs, share_ref = refs[-1 - channels : -1], refs[-1]
    means = [mean_ref[s_ref[2 + step], start : start + rows] for step, start, rows, _ in unit]
    for c in range(channels):
        mean = stacked([column[:, c : c + 1] for column in means])
        for x in range(across):
            capped_refs[c][x] = 2.0 * jnp.tanh((sums_ref[c, x] + more_ref[c, x] - mean) / 2.0)
        at = 0
        for step, start, rows, shard in unit:
            to = pl.ds(pl.multiple_of(s_ref[2 + step] * shard + start, 8), rows)
            share_ref[c, to, :] = capped_refs[c][s_ref[1], at : at + rows]
            at += rows


def cap(unit, scalars, means, sums, more, share, all_fields):
    channels, _, _, rows = sums.shape
    operands = [scalars, means, sums, more]
    in_specs = [pl.BlockSpec(memory_space=pltpu.SMEM), WHOLE, WHOLE, WHOLE]
    aliases = {}
    if share is not None:
        aliases = {len(operands): channels}
        operands.append(share)
        in_specs.append(WHOLE)
    return pl.pallas_call(
        functools.partial(cap_kernel, unit),
        out_shape=[jax.ShapeDtypeStruct(sums.shape[1:], jnp.float32)] * channels
        + [pltpu.VMEM((channels, all_fields, rows), jnp.float32)],
        in_specs=in_specs,
        out_specs=[WHOLE] * (channels + 1),
        input_output_aliases=aliases,
        compiler_params=params(8),
        cost_estimate=COST,
        name="cap",
    )(*operands)


def stack_chol(out, parts):
    high, low = split(stacked([part[...] for part in parts]))
    depth = high.shape[0]
    out[:depth] = high
    out[depth : 2 * depth] = high
    out[2 * depth :] = low


def stack_fields(capped, noise):
    first = stacked(noise) - stacked(capped[0::2])
    second = -stacked(capped[1::2])
    high, low = split(jnp.concatenate([first, second], 1))
    return jnp.concatenate([high, low, high], 0).T


def noise_specs(unit, noise, lanes, rows):
    apart, blocks = noise.shape[1] > 1, rows // lanes

    def spec(step, shard):
        def at(x, h, b, s):
            share = x * CORES + h
            return (s[2 + step], share, 0, b) if apart else (s[2 + step], 0, 0, share * blocks + b)

        return pl.BlockSpec((1, 1, shard, lanes), at)

    return [spec(step, shard) for step, _, _, shard in unit]


def noise_pieces(refs, unit):
    return [ref[0, 0, start : start + rows] for ref, (_, start, rows, _) in zip(refs, unit)]


def stack_kernel(*refs):
    stack_chol(refs[-1], refs[:-1])


def stack_of(chol):
    depth = sum(part.shape[0] for part in chol)
    return pl.pallas_call(
        stack_kernel,
        out_shape=pltpu.VMEM((3 * depth, chol[0].shape[1]), jnp.bfloat16),
        in_specs=[WHOLE] * len(chol),
        out_specs=WHOLE,
        compiler_params=params(12),
        cost_estimate=COST,
        name="stack_cholesky",
    )(*chol)


def begin_kernel(n, unit, s_ref, *refs):
    mine, other, noise, (stack, out_ref) = refs[:n], refs[n : 2 * n], refs[2 * n : -2], refs[-2:]
    x, core = pl.program_id(0), pl.program_id(1)
    own = core == s_ref[0]
    capped = [jnp.where(own, a[0], b[0]) for a, b in zip(mine, other)]
    out_ref[x, core] = lax.dot_general(
        stack_fields(capped, noise_pieces(noise, unit)), stack[...], DOT, preferred_element_type=jnp.float32
    )


def begin(mine, other, noise, stack, unit, scalars, sizes):
    across, rows, pairs = sizes
    in_specs = [pl.BlockSpec((1, *part.shape[1:]), lambda x, h, s: (x, 0, 0)) for part in (*mine, *other)]
    in_specs += [
        pl.BlockSpec(spec.block_shape, lambda x, h, s, at=spec.index_map: at(x, h, 0, s))
        for spec in noise_specs(unit, noise, rows, rows)
    ]
    return pl.pallas_call(
        functools.partial(begin_kernel, len(mine), unit),
        out_shape=pltpu.VMEM((across, CORES, 2 * rows, pairs), jnp.float32),
        grid_spec=pltpu.PrefetchScalarGridSpec(
            num_scalar_prefetch=1, grid=(across, CORES), in_specs=[*in_specs, WHOLE], out_specs=WHOLE
        ),
        compiler_params=params(16),
        cost_estimate=COST,
        name="begin",
    )(scalars, *mine, *other, *([noise] * len(unit)), stack)


def finish_kernel(n, m, unit, scale, s_ref, *refs):
    mine, other, noise = refs[:n], refs[n : 2 * n], refs[2 * n : 2 * n + m]
    stack, prior, share, out_ref, turned_ref, left = refs[2 * n + m :]
    turn, x, p = pl.program_id(0), pl.program_id(1), pl.program_id(2)
    core = (s_ref[0] + turn) % CORES

    @pl.when((turn == 0) & (x == 0) & (p == 0))
    def _():
        for c in range(2):
            turned_ref[c] = share[c].T

    @pl.when(p == 0)
    def _():
        capped = [jnp.where(turn == 0, a[0], b[0]) for a, b in zip(mine, other)]
        left[...] = stack_fields(capped, noise_pieces(noise, unit))

    width = out_ref.shape[-1]
    columns = pl.ds(pl.multiple_of(p * width, 128), width)
    sums = lax.dot_general(left[...], stack[:, columns], DOT, preferred_element_type=jnp.float32)
    rows = sums.shape[0] // 2
    for c in range(2):
        part = slice(c * rows, (c + 1) * rows)
        out_ref[0, 0, :, c, :] = scale * (prior[x, core, part, columns] + sums[part])


def finish(mine, other, noise, stack, prior, share, unit, scalars, scale, sizes):
    across, rows, pairs = sizes
    tiles = 3 if pairs % 384 == 0 else 1
    turned = (share.shape[0], share.shape[2], share.shape[1])
    in_specs = [pl.BlockSpec((1, *part.shape[1:]), lambda t, x, p, s: (x, 0, 0)) for part in (*mine, *other)]
    in_specs += [
        pl.BlockSpec(spec.block_shape, lambda t, x, p, s, at=spec.index_map: at(x, (s[0] + t) % CORES, 0, s))
        for spec in noise_specs(unit, noise, rows, rows)
    ]
    return pl.pallas_call(
        functools.partial(finish_kernel, len(mine), len(unit), unit, scale),
        out_shape=[
            jax.ShapeDtypeStruct((across, CORES, rows, 2, pairs), jnp.float32),
            jax.ShapeDtypeStruct(turned, jnp.float32),
        ],
        grid_spec=pltpu.PrefetchScalarGridSpec(
            num_scalar_prefetch=1,
            grid=(CORES, across, tiles),
            in_specs=[*in_specs, WHOLE, WHOLE, WHOLE],
            out_specs=[
                pl.BlockSpec(
                    (1, 1, rows, 2, pairs // tiles), lambda t, x, p, s: (x, (s[0] + t) % CORES, 0, 0, p)
                ),
                pl.BlockSpec(turned, lambda t, x, p, s: (0, 0, 0)),
            ],
            scratch_shapes=[pltpu.VMEM((2 * rows, stack.shape[0]), jnp.bfloat16)],
        ),
        compiler_params=params(16),
        cost_estimate=COST,
        name="finish",
    )(scalars, *mine, *other, *([noise] * len(unit)), stack, prior, share)


def after(x, *earlier):
    return lax.optimization_barrier((x, *earlier))[0]


def per_device(ring_size, pair_size, cholesky_tensor, green_function, mean_field, field_noise):
    shard, pairs = cholesky_tensor.shape
    channels, walkers, _ = green_function.shape
    fields = ring_size * shard
    total_pairs = pair_size * pairs
    across = pair_size // CORES
    rows = walkers // pair_size
    sizes = (across, rows, pairs)
    scale = math.sqrt(total_pairs / fields)

    place, member = lax.axis_index("field"), lax.axis_index("pair")
    core, chip = member % CORES, member // CORES
    owners = [(place - step) % ring_size for step in range(ring_size)]
    own_scalars = jnp.stack([core, chip, *owners]).astype(jnp.int32)
    mate_scalars = jnp.stack([1 - core, chip, *owners]).astype(jnp.int32)

    ring = [(i, (i + 1) % ring_size) for i in range(ring_size)]
    mates = [(i, i ^ 1) for i in range(pair_size)]

    count = 2 if shard % 32 == 0 and ring_size > 2 else 1
    cuts = [(i * (shard // count), shard // count) for i in range(count)]
    pieces = [(step, start, n, shard) for step in range(1, ring_size) for start, n in cuts]
    held, cut = {}, cholesky_tensor
    for start, n in cuts:
        held[0, start] = lax.slice_in_dim(cut, start, start + n, axis=0)
        cut = lax.optimization_barrier((cut, held[0, start]))[0]

    own_piece = (0, 0, shard, shard)
    if count > 1:
        units = [[own_piece]] + [pieces[i : i + 2] for i in range(0, len(pieces) - 2, 2)] + [[p] for p in pieces[-2:]]
    else:
        run = 1
        while run * shard % 16 or run * 8 < ring_size:
            run *= 2
        line = [own_piece, *pieces]
        units = [line[i : i + run] for i in range(0, len(line), run)]
    n_units = len(units)

    def hop(step, start, token):
        held[step, start] = lax.ppermute(after(held[step - 1, start], *token), "field", ring)

    def parts_of(unit):
        return [cholesky_tensor if piece == own_piece else held[piece[0], piece[1]] for piece in unit]

    for start, _ in cuts:
        hop(1, start, ())
    green = green_function.reshape(channels, across, CORES, rows, pairs)
    turned = field_noise.T
    if rows % 128:
        noise = turned.reshape(ring_size, shard, pair_size, rows).transpose(0, 2, 1, 3)
    else:
        noise = turned.reshape(ring_size, 1, shard, walkers)
    means = mean_field.T.reshape(ring_size, shard, channels)
    ready = [held[0, start] for start, _ in cuts] + [noise, means, mate_scalars]
    own_high, own_low, mate_high, mate_low = split_green(after(own_scalars, *ready), green)
    state = {"share": None, "token": ()}
    fronts, sums, own, mate = {}, {}, {}, {}

    def front(u):
        parts = parts_of(units[u])
        parts[0] = after(parts[0], *state["token"])
        sent = bias_of(mate_high, mate_low, parts)
        arrived = [lax.ppermute(part, "pair", mates) for part in sent]
        kept = bias_of(own_high, own_low, [after(parts[0], *sent), *parts[1:]])
        state["token"] = tuple(kept)
        fronts[u] = (kept, arrived)

    def across_chips(u):
        kept, arrived = fronts[u]
        total = add(kept, arrived)
        reach = CORES
        while 2 * reach < pair_size:
            more = lax.ppermute(total, "pair", [(i, i ^ reach) for i in range(pair_size)])
            total = add([total[c] for c in range(channels)], [more[c] for c in range(channels)])
            reach *= 2
        sums[u] = (total, lax.ppermute(total, "pair", [(i, i ^ reach) for i in range(pair_size)]))

    def back(u, tie=()):
        total, more = sums[u]
        *own[u], state["share"] = cap(
            units[u], own_scalars, after(means, *tie), total, more, state["share"], fields
        )
        mate[u] = [lax.ppermute(part, "pair", mates) for part in own[u]]

    def send_on(piece):
        step, start, _, _ = piece
        arrived = held[step, start]
        if step + 1 < ring_size:
            hop(step + 1, start, state["token"])
        state["token"] = (*state["token"], arrived)

    if count > 1:
        front(0)
        across_chips(0)
        for step in range(1, ring_size):
            send_on(pieces[2 * step - 2])
            if step + 1 == ring_size:
                front(n_units - 2)
            state["token"] += (sums[step - 1][0],) + ((own[step - 2][0],) if step > 1 else ())
            send_on(pieces[2 * step - 1])
            if step + 1 < ring_size:
                front(step)
                across_chips(step)
                back(step - 1)
        across_chips(n_units - 2)
        state["token"] += (sums[n_units - 2][0],)
        front(n_units - 1)
        across_chips(n_units - 1)
        state["token"] += (sums[n_units - 1][0],)
        final = 3
    else:
        for u, unit in enumerate(units):
            for piece in unit:
                if piece != own_piece:
                    send_on(piece)
            front(u)
            across_chips(u)
            if u:
                back(u - 1)
        state["token"] += (sums[n_units - 1][0],)
        final = 1

    def stack_and_pieces(chosen):
        parts = [part for u in chosen for part in parts_of(units[u])]
        return stack_of([after(parts[0], *state["token"]), *parts[1:]]), [piece for u in chosen for piece in units[u]]

    def channels_of(capped, chosen):
        return [part for u in chosen for part in capped[u]]

    first, late = range(n_units - final), range(n_units - final, n_units)
    stack, line = stack_and_pieces(first)
    operator = begin(channels_of(own, first), channels_of(mate, first), noise, stack, line, own_scalars, sizes)
    stack, line = stack_and_pieces(late)
    for u in late:
        if u not in own:
            back(u, (operator, stack))
    one_body, capped = finish(
        channels_of(own, late), channels_of(mate, late), noise, stack, operator, state["share"], line, own_scalars,
        scale, sizes,
    )
    return (capped, one_body.reshape(walkers, channels, pairs))


def solution(mesh):
    return jax.shard_map(
        functools.partial(per_device, mesh.shape["field"], mesh.shape["pair"]),
        mesh=mesh,
        in_specs=(
            P(("grp", "field"), "pair"),
            P(None, ("grp", "field"), "pair"),
            P(None, "grp"),
            P(("grp", "field"), None),
        ),
        out_specs=(P(None, ("grp", "field", "pair"), None), P(("grp", "field"), None, "pair")),
        check_vma=False,
    )
```

```python
import functools
import math

import jax
import jax.numpy as jnp
from jax import lax
from jax.experimental import pallas as pl
from jax.experimental.pallas import tpu as pltpu
from jax.sharding import PartitionSpec as P

CORES = 2
MIB = 1024 * 1024
ROWS_DOT = (((1,), (1,)), ((), ()))
DOT = (((1,), (0,)), ((), ()))
WHOLE = pl.BlockSpec(memory_space=pltpu.VMEM)
COST = pl.CostEstimate(flops=1, bytes_accessed=1, transcendentals=0)


def split(x):
    high = x.astype(jnp.bfloat16)
    return high, (x - high.astype(jnp.float32)).astype(jnp.bfloat16)


def params(mib):
    return pltpu.CompilerParams(vmem_limit_bytes=mib * MIB)


def stacked(parts):
    return parts[0] if len(parts) == 1 else jnp.concatenate(parts, 0)


def split_green_kernel(s_ref, green_ref, own_high_ref, own_low_ref, mate_high_ref, mate_low_ref):
    at = (pl.program_id(0), pl.program_id(1))
    high, low = split(green_ref[0, 0, 0])
    own = pl.program_id(2) == s_ref[0]

    @pl.when(own)
    def _():
        own_high_ref[at], own_low_ref[at] = high, low

    @pl.when(jnp.logical_not(own))
    def _():
        mate_high_ref[at], mate_low_ref[at] = high, low


def split_green(scalars, green):
    channels, across, cores, rows, pairs = green.shape
    return pl.pallas_call(
        split_green_kernel,
        out_shape=[pltpu.VMEM((channels, across, rows, pairs), jnp.bfloat16)] * 4,
        grid=(channels, across, cores),
        in_specs=[
            pl.BlockSpec(memory_space=pltpu.SMEM),
            pl.BlockSpec((1, 1, 1, rows, pairs), lambda c, x, h: (c, x, h, 0, 0)),
        ],
        out_specs=[WHOLE] * 4,
        compiler_params=params(12),
        cost_estimate=COST,
        name="split_green",
    )(scalars, green)


def bias_kernel(n, high_ref, low_ref, *refs):
    parts, out_refs, chol = refs[:n], refs[n:-1], refs[-1]
    fields = chol.shape[0] // 2
    chol[:fields], chol[fields:] = split(stacked([part[...] for part in parts]))
    channels, across = high_ref.shape[:2]
    for c in range(channels):
        for x in range(across):
            both = lax.dot_general(chol[...], high_ref[c, x], ROWS_DOT, preferred_element_type=jnp.float32)
            cross = lax.dot_general(chol[:fields], low_ref[c, x], ROWS_DOT, preferred_element_type=jnp.float32)
            out_refs[c][x] = both[:fields] + (both[fields:] + cross)


def bias_of(high, low, parts):
    channels, across, rows, pairs = high.shape
    fields = sum(part.shape[0] for part in parts)
    return pl.pallas_call(
        functools.partial(bias_kernel, len(parts)),
        out_shape=[jax.ShapeDtypeStruct((across, fields, rows), jnp.float32)] * channels,
        in_specs=[WHOLE] * (2 + len(parts)),
        out_specs=[WHOLE] * channels,
        scratch_shapes=[pltpu.VMEM((2 * fields, pairs), jnp.bfloat16)],
        compiler_params=params(10),
        cost_estimate=COST,
        name="bias",
    )(high, low, *parts)


def add_kernel(n, *refs):
    for c in range(n):
        refs[-1][c] = refs[c][...] + refs[n + c][...]


def add(a, b):
    return pl.pallas_call(
        functools.partial(add_kernel, len(a)),
        out_shape=jax.ShapeDtypeStruct((len(a), *a[0].shape), a[0].dtype),
        in_specs=[WHOLE] * (2 * len(a)),
        out_specs=WHOLE,
        compiler_params=params(6),
        cost_estimate=COST,
        name="add",
    )(*a, *b)


def cap_kernel(unit, s_ref, mean_ref, sums_ref, more_ref, *refs):
    channels, across, fields, _ = sums_ref.shape
    capped_refs, share_ref = refs[-1 - channels : -1], refs[-1]
    means = [mean_ref[s_ref[2 + step], start : start + rows] for step, start, rows, _ in unit]
    for c in range(channels):
        mean = stacked([column[:, c : c + 1] for column in means])
        for x in range(across):
            capped_refs[c][x] = 2.0 * jnp.tanh((sums_ref[c, x] + more_ref[c, x] - mean) / 2.0)
        at = 0
        for step, start, rows, shard in unit:
            to = pl.ds(pl.multiple_of(s_ref[2 + step] * shard + start, 8), rows)
            share_ref[c, to, :] = capped_refs[c][s_ref[1], at : at + rows]
            at += rows


def cap(unit, scalars, means, sums, more, share, all_fields):
    channels, _, _, rows = sums.shape
    operands = [scalars, means, sums, more]
    in_specs = [pl.BlockSpec(memory_space=pltpu.SMEM), WHOLE, WHOLE, WHOLE]
    aliases = {}
    if share is not None:
        aliases = {len(operands): channels}
        operands.append(share)
        in_specs.append(WHOLE)
    return pl.pallas_call(
        functools.partial(cap_kernel, unit),
        out_shape=[jax.ShapeDtypeStruct(sums.shape[1:], jnp.float32)] * channels
        + [pltpu.VMEM((channels, all_fields, rows), jnp.float32)],
        in_specs=in_specs,
        out_specs=[WHOLE] * (channels + 1),
        input_output_aliases=aliases,
        compiler_params=params(8),
        cost_estimate=COST,
        name="cap",
    )(*operands)


def stack_chol(out, parts):
    high, low = split(stacked([part[...] for part in parts]))
    depth = high.shape[0]
    out[:depth] = high
    out[depth : 2 * depth] = high
    out[2 * depth :] = low


def stack_fields(capped, noise):
    first = stacked(noise) - stacked(capped[0::2])
    second = -stacked(capped[1::2])
    high, low = split(jnp.concatenate([first, second], 1))
    return jnp.concatenate([high, low, high], 0).T


def noise_specs(unit, noise, lanes, rows):
    apart, blocks = noise.shape[1] > 1, rows // lanes

    def spec(step, shard):
        def at(x, h, b, s):
            share = x * CORES + h
            return (s[2 + step], share, 0, b) if apart else (s[2 + step], 0, 0, share * blocks + b)

        return pl.BlockSpec((1, 1, shard, lanes), at)

    return [spec(step, shard) for step, _, _, shard in unit]


def noise_pieces(refs, unit):
    return [ref[0, 0, start : start + rows] for ref, (_, start, rows, _) in zip(refs, unit)]


def stack_kernel(*refs):
    stack_chol(refs[-1], refs[:-1])


def stack_of(chol):
    depth = sum(part.shape[0] for part in chol)
    return pl.pallas_call(
        stack_kernel,
        out_shape=pltpu.VMEM((3 * depth, chol[0].shape[1]), jnp.bfloat16),
        in_specs=[WHOLE] * len(chol),
        out_specs=WHOLE,
        compiler_params=params(12),
        cost_estimate=COST,
        name="stack_cholesky",
    )(*chol)


def begin_kernel(n, unit, s_ref, *refs):
    mine, other, noise, (stack, out_ref) = refs[:n], refs[n : 2 * n], refs[2 * n : -2], refs[-2:]
    x, core = pl.program_id(0), pl.program_id(1)
    own = core == s_ref[0]
    capped = [jnp.where(own, a[0], b[0]) for a, b in zip(mine, other)]
    out_ref[x, core] = lax.dot_general(
        stack_fields(capped, noise_pieces(noise, unit)), stack[...], DOT, preferred_element_type=jnp.float32
    )


def begin(mine, other, noise, stack, unit, scalars, sizes):
    across, rows, pairs = sizes
    in_specs = [pl.BlockSpec((1, *part.shape[1:]), lambda x, h, s: (x, 0, 0)) for part in (*mine, *other)]
    in_specs += [
        pl.BlockSpec(spec.block_shape, lambda x, h, s, at=spec.index_map: at(x, h, 0, s))
        for spec in noise_specs(unit, noise, rows, rows)
    ]
    return pl.pallas_call(
        functools.partial(begin_kernel, len(mine), unit),
        out_shape=pltpu.VMEM((across, CORES, 2 * rows, pairs), jnp.float32),
        grid_spec=pltpu.PrefetchScalarGridSpec(
            num_scalar_prefetch=1, grid=(across, CORES), in_specs=[*in_specs, WHOLE], out_specs=WHOLE
        ),
        compiler_params=params(16),
        cost_estimate=COST,
        name="begin",
    )(scalars, *mine, *other, *([noise] * len(unit)), stack)


def finish_kernel(n, m, unit, scale, s_ref, *refs):
    mine, other, noise = refs[:n], refs[n : 2 * n], refs[2 * n : 2 * n + m]
    stack, prior, share, out_ref, turned_ref, left = refs[2 * n + m :]
    turn, x, p = pl.program_id(0), pl.program_id(1), pl.program_id(2)
    core = (s_ref[0] + turn) % CORES

    @pl.when((turn == 0) & (x == 0) & (p == 0))
    def _():
        for c in range(2):
            turned_ref[c] = share[c].T

    @pl.when(p == 0)
    def _():
        capped = [jnp.where(turn == 0, a[0], b[0]) for a, b in zip(mine, other)]
        left[...] = stack_fields(capped, noise_pieces(noise, unit))

    width = out_ref.shape[-1]
    columns = pl.ds(pl.multiple_of(p * width, 128), width)
    sums = lax.dot_general(left[...], stack[:, columns], DOT, preferred_element_type=jnp.float32)
    rows = sums.shape[0] // 2
    for c in range(2):
        part = slice(c * rows, (c + 1) * rows)
        out_ref[0, 0, :, c, :] = scale * (prior[x, core, part, columns] + sums[part])


def finish(mine, other, noise, stack, prior, share, unit, scalars, scale, sizes):
    across, rows, pairs = sizes
    tiles = 2 if pairs % 256 == 0 else 1
    turned = (share.shape[0], share.shape[2], share.shape[1])
    in_specs = [pl.BlockSpec((1, *part.shape[1:]), lambda t, x, p, s: (x, 0, 0)) for part in (*mine, *other)]
    in_specs += [
        pl.BlockSpec(spec.block_shape, lambda t, x, p, s, at=spec.index_map: at(x, (s[0] + t) % CORES, 0, s))
        for spec in noise_specs(unit, noise, rows, rows)
    ]
    return pl.pallas_call(
        functools.partial(finish_kernel, len(mine), len(unit), unit, scale),
        out_shape=[
            jax.ShapeDtypeStruct((across, CORES, rows, 2, pairs), jnp.float32),
            jax.ShapeDtypeStruct(turned, jnp.float32),
        ],
        grid_spec=pltpu.PrefetchScalarGridSpec(
            num_scalar_prefetch=1,
            grid=(CORES, across, tiles),
            in_specs=[*in_specs, WHOLE, WHOLE, WHOLE],
            out_specs=[
                pl.BlockSpec(
                    (1, 1, rows, 2, pairs // tiles), lambda t, x, p, s: (x, (s[0] + t) % CORES, 0, 0, p)
                ),
                pl.BlockSpec(turned, lambda t, x, p, s: (0, 0, 0)),
            ],
            scratch_shapes=[pltpu.VMEM((2 * rows, stack.shape[0]), jnp.bfloat16)],
        ),
        compiler_params=params(16),
        cost_estimate=COST,
        name="finish",
    )(scalars, *mine, *other, *([noise] * len(unit)), stack, prior, share)


def after(x, *earlier):
    return lax.optimization_barrier((x, *earlier))[0]


def per_device(ring_size, pair_size, cholesky_tensor, green_function, mean_field, field_noise):
    shard, pairs = cholesky_tensor.shape
    channels, walkers, _ = green_function.shape
    fields = ring_size * shard
    total_pairs = pair_size * pairs
    across = pair_size // CORES
    rows = walkers // pair_size
    sizes = (across, rows, pairs)
    scale = math.sqrt(total_pairs / fields)

    place, member = lax.axis_index("field"), lax.axis_index("pair")
    core, chip = member % CORES, member // CORES
    owners = [(place - step) % ring_size for step in range(ring_size)]
    own_scalars = jnp.stack([core, chip, *owners]).astype(jnp.int32)
    mate_scalars = jnp.stack([1 - core, chip, *owners]).astype(jnp.int32)

    ring = [(i, (i + 1) % ring_size) for i in range(ring_size)]
    mates = [(i, i ^ 1) for i in range(pair_size)]

    count = 2 if shard % 32 == 0 and ring_size > 2 else 1
    cuts = [(i * (shard // count), shard // count) for i in range(count)]
    pieces = [(step, start, n, shard) for step in range(1, ring_size) for start, n in cuts]
    held, cut = {}, cholesky_tensor
    for start, n in cuts:
        held[0, start] = lax.slice_in_dim(cut, start, start + n, axis=0)
        cut = lax.optimization_barrier((cut, held[0, start]))[0]

    own_piece = (0, 0, shard, shard)
    if count > 1:
        units = [[own_piece]] + [pieces[i : i + 2] for i in range(0, len(pieces) - 2, 2)] + [[p] for p in pieces[-2:]]
    else:
        run = 1
        while run * shard % 16 or run * 8 < ring_size:
            run *= 2
        line = [own_piece, *pieces]
        units = [line[i : i + run] for i in range(0, len(line), run)]
    n_units = len(units)

    def hop(step, start, token):
        held[step, start] = lax.ppermute(after(held[step - 1, start], *token), "field", ring)

    def parts_of(unit):
        return [cholesky_tensor if piece == own_piece else held[piece[0], piece[1]] for piece in unit]

    for start, _ in cuts:
        hop(1, start, ())
    green = green_function.reshape(channels, across, CORES, rows, pairs)
    turned = field_noise.T
    if rows % 128:
        noise = turned.reshape(ring_size, shard, pair_size, rows).transpose(0, 2, 1, 3)
    else:
        noise = turned.reshape(ring_size, 1, shard, walkers)
    means = mean_field.T.reshape(ring_size, shard, channels)
    ready = [held[0, start] for start, _ in cuts] + [noise, means, mate_scalars]
    own_high, own_low, mate_high, mate_low = split_green(after(own_scalars, *ready), green)
    state = {"share": None, "token": ()}
    fronts, sums, own, mate = {}, {}, {}, {}

    def front(u):
        parts = parts_of(units[u])
        parts[0] = after(parts[0], *state["token"])
        sent = bias_of(mate_high, mate_low, parts)
        arrived = [lax.ppermute(part, "pair", mates) for part in sent]
        kept = bias_of(own_high, own_low, [after(parts[0], *sent), *parts[1:]])
        state["token"] = tuple(kept)
        fronts[u] = (kept, arrived)

    def across_chips(u):
        kept, arrived = fronts[u]
        total = add(kept, arrived)
        reach = CORES
        while 2 * reach < pair_size:
            more = lax.ppermute(total, "pair", [(i, i ^ reach) for i in range(pair_size)])
            total = add([total[c] for c in range(channels)], [more[c] for c in range(channels)])
            reach *= 2
        sums[u] = (total, lax.ppermute(total, "pair", [(i, i ^ reach) for i in range(pair_size)]))

    def back(u, tie=()):
        total, more = sums[u]
        *own[u], state["share"] = cap(
            units[u], own_scalars, after(means, *tie), total, more, state["share"], fields
        )
        mate[u] = [lax.ppermute(part, "pair", mates) for part in own[u]]

    def send_on(piece):
        step, start, _, _ = piece
        arrived = held[step, start]
        if step + 1 < ring_size:
            hop(step + 1, start, state["token"])
        state["token"] = (*state["token"], arrived)

    if count > 1:
        front(0)
        across_chips(0)
        for step in range(1, ring_size):
            send_on(pieces[2 * step - 2])
            if step + 1 == ring_size:
                front(n_units - 2)
            state["token"] += (sums[step - 1][0],) + ((own[step - 2][0],) if step > 1 else ())
            send_on(pieces[2 * step - 1])
            if step + 1 < ring_size:
                front(step)
                across_chips(step)
                back(step - 1)
        across_chips(n_units - 2)
        state["token"] += (sums[n_units - 2][0],)
        front(n_units - 1)
        across_chips(n_units - 1)
        state["token"] += (sums[n_units - 1][0],)
        final = 3
    else:
        for u, unit in enumerate(units):
            for piece in unit:
                if piece != own_piece:
                    send_on(piece)
            front(u)
            across_chips(u)
            if u:
                back(u - 1)
        state["token"] += (sums[n_units - 1][0],)
        final = 1

    def stack_and_pieces(chosen):
        parts = [part for u in chosen for part in parts_of(units[u])]
        return stack_of([after(parts[0], *state["token"]), *parts[1:]]), [piece for u in chosen for piece in units[u]]

    def channels_of(capped, chosen):
        return [part for u in chosen for part in capped[u]]

    first, late = range(n_units - final), range(n_units - final, n_units)
    stack, line = stack_and_pieces(first)
    operator = begin(channels_of(own, first), channels_of(mate, first), noise, stack, line, own_scalars, sizes)
    stack, line = stack_and_pieces(late)
    for u in late:
        if u not in own:
            back(u, (operator, stack))
    one_body, capped = finish(
        channels_of(own, late), channels_of(mate, late), noise, stack, operator, state["share"], line, own_scalars,
        scale, sizes,
    )
    return (capped, one_body.reshape(walkers, channels, pairs))


def solution(mesh):
    return jax.shard_map(
        functools.partial(per_device, mesh.shape["field"], mesh.shape["pair"]),
        mesh=mesh,
        in_specs=(
            P(("grp", "field"), "pair"),
            P(None, ("grp", "field"), "pair"),
            P(None, "grp"),
            P(("grp", "field"), None),
        ),
        out_specs=(P(None, ("grp", "field", "pair"), None), P(("grp", "field"), None, "pair")),
        check_vma=False,
    )
```
